128 devices in a mesh: wall: 4 (over y), span: 32 (over x, z, core).
Axes of the slice: x: 4, y: 4, z: 4, core: 2. Of those that a mesh axis runs over, the one named last changes fastest.
Arguments:
- jac_lower: bfloat16 [8, 112, 112, 4096], P('wall', None, None, 'span')
- jac_inv_diag: bfloat16 [8, 112, 112, 4096], P('wall', None, None, 'span')
- jac_upper: bfloat16 [8, 112, 112, 4096], P('wall', None, None, 'span')
- residual: float32 [8, 112, 4096], P('wall', None, 'span'), may hold values from -6 to 6
- prev_update: float32 [8, 112, 4096], P('wall', None, 'span'), may hold values from -6 to 6
- send_lines: int32 [32, 32, 64], P('span'), may hold values from 0 to 127
- send_count: int32 [32, 32], P('span'), may hold values from 1 to 64, as said below
- recv_lines: int32 [32, 32, 64], P('span'), may hold values from 0 to 127
- active_lines: int32 [32], P('span'), may hold values from 64 to 128, as said below
Outputs:
- line_update: float32 [8, 112, 4096], P('wall', None, 'span')
The draws below stay inside these ranges and needn't reach their ends.
Inputs may be any that keep to these rules, and one draw needn't show every extreme that they name: `send_count`: every sender fills all 64 slots towards at least one receiver, and one receiver gets full slots from every sender. `active_lines`: at least one device has all 128 lines live.
All inputs are finite; a program needn't handle non-finite values.
Results may differ from the reference program's by a relative error of at most 0.0003.
Values sent between devices are 32-bit elements; how exact they have to be, the bound alone decides.
A program may use at most 256 MiB of HBM per device.

```python
import math
import jax
import jax.numpy as jnp
from jax import lax

NC = 112
LD = 128
SLOTS = 64
NW = 8
LINES = 4096
N_SPAN = 32


def factor_block(key, low, high, sign):
    key_diag, key_off = jax.random.split(key)
    diag = jnp.exp(jax.random.uniform(key_diag, (NW, NC, LINES), jnp.float32, math.log(low), math.log(high)))
    off = jax.random.normal(key_off, (NW, NC, NC, LINES), jnp.float32) * (0.25 / math.sqrt(NC))
    ident = (jnp.arange(NC)[:, None] == jnp.arange(NC)[None, :]).astype(jnp.float32)
    return (sign * (off + ident[None, :, :, None] * diag[:, :, None, :])).astype(jnp.bfloat16)


def draw_jac_lower(key, part):
    return factor_block(jax.random.fold_in(key, 11), 0.5, 1.0, -1.0)


def draw_jac_inv_diag(key, part):
    return factor_block(jax.random.fold_in(key, 12), 0.5, 2.0, 1.0)


def draw_jac_upper(key, part):
    return factor_block(jax.random.fold_in(key, 13), 0.5, 1.0, -1.0)


def draw_send_count(key, part):
    key_count, key_full = jax.random.split(jax.random.fold_in(key, 21))
    counts = jax.random.randint(key_count, (N_SPAN, N_SPAN), 1, SLOTS + 1)
    column = jax.random.randint(key_full, (), 0, N_SPAN)
    full = jnp.arange(N_SPAN)[None, :] == column
    return jnp.where(full, SLOTS, counts).astype(jnp.int32)


def draw_active_lines(key, part):
    key_count, key_full = jax.random.split(jax.random.fold_in(key, 31))
    counts = jax.random.randint(key_count, (N_SPAN,), LD // 2, LD + 1)
    which = jax.random.randint(key_full, (), 0, N_SPAN)
    return jnp.where(jnp.arange(N_SPAN) == which, LD, counts).astype(jnp.int32)


def place_ends(values, key, smallest, largest):
    longest = values.shape.index(max(values.shape))
    spots = []
    for shift in (0, 1):
        where = [jax.random.randint(jax.random.fold_in(key, axis), (), 0, length) for axis, length in enumerate(values.shape)]
        where[longest] = (where[longest] + shift) % values.shape[longest]
        spots.append(tuple(where))
    return values.at[spots[0]].set(smallest).at[spots[1]].set(largest)


def block_levels(own_key, dims, shards, least, high):
    factor_of = 1.0
    for position, blocks in shards:
        draws = jax.random.uniform(jax.random.fold_in(jax.random.fold_in(own_key, 6), position), (blocks,), jnp.float32, least / len(shards), high / len(shards))
        factor_of = factor_of * jnp.repeat(jnp.exp(draws), dims[position] // blocks).reshape((-1,) + (1,) * (len(dims) - 1 - position))
    return factor_of


def scatter_about(stream_key, shape, width, limit, cuts=(), held_as=jnp.bfloat16):
    values = width * jax.random.normal(stream_key, shape, jnp.float32)
    if cuts:
        values = values * block_levels(stream_key, shape, cuts, -0.22, 0.18)
    return jnp.clip(values, -limit, limit).astype(held_as)


def setup_inputs(seed: int = 0) -> dict:
    arg_keys = jax.random.split(jax.random.key(seed), 10)
    return {
        "jac_lower": draw_jac_lower(jax.random.fold_in(arg_keys[9], 71), 0),
        "jac_inv_diag": draw_jac_inv_diag(jax.random.fold_in(arg_keys[9], 71), 0),
        "jac_upper": draw_jac_upper(jax.random.fold_in(arg_keys[9], 71), 0),
        "residual": scatter_about(arg_keys[3], (NW, NC, LINES), 1.0, 6.0, ((0, 4), (2, 32)), jnp.float32),
        "prev_update": scatter_about(arg_keys[4], (NW, NC, LINES), 1.0, 6.0, ((0, 4), (2, 32)), jnp.float32),
        "send_lines": place_ends(jax.random.randint(arg_keys[5], (N_SPAN, N_SPAN, SLOTS), 0, LD), jax.random.fold_in(arg_keys[5], 1), 0, LD - 1).astype(jnp.int32),
        "send_count": draw_send_count(jax.random.fold_in(arg_keys[9], 71), 0),
        "recv_lines": place_ends(jax.random.randint(arg_keys[7], (N_SPAN, N_SPAN, SLOTS), 0, LD), jax.random.fold_in(arg_keys[7], 1), 0, LD - 1).astype(jnp.int32),
        "active_lines": draw_active_lines(jax.random.fold_in(arg_keys[9], 71), 0),
    }


def matvec(block, vec):
    return jnp.einsum("abl,bl->al", block.astype(jnp.float32), vec, precision=lax.Precision.HIGHEST)


def lower_sweep(jac_lower, rhs, start_vec):
    def step(carry, inputs):
        block, right = inputs
        value = right - matvec(block, carry)
        return value, value
    last, values = lax.scan(step, start_vec, (jac_lower, rhs))
    return last, values


def upper_sweep(jac_inv_diag, jac_upper, values, start_vec):
    def step(carry, inputs):
        inverse, block, right = inputs
        value = matvec(inverse, right - matvec(block, carry))
        return value, value
    first, result = lax.scan(step, start_vec, (jac_inv_diag, jac_upper, values), reverse=True)
    return first, result


def reference(jac_lower, jac_inv_diag, jac_upper, residual, prev_update, send_lines, send_count, recv_lines, active_lines):
    slot_ids = jnp.arange(SLOTS, dtype=jnp.int32)
    recv_ids = jnp.arange(N_SPAN, dtype=jnp.int32)

    def add_source(source, total):
        lines_here = send_lines[source]
        keep = (slot_ids[None, :] < send_count[source][:, None]) & (lines_here < active_lines[source])
        src = (source * LD + lines_here).reshape(-1).astype(jnp.int32)
        dst = (recv_ids[:, None] * LD + recv_lines[:, source, :]).reshape(-1).astype(jnp.int32)
        vals = prev_update[:, :, src] * keep.reshape(-1).astype(jnp.float32)
        return total.at[:, :, dst].add(vals)

    coupling = lax.fori_loop(0, N_SPAN, add_source, jnp.zeros(residual.shape, jnp.float32))
    line_ids = jnp.arange(LINES, dtype=jnp.int32)
    live = (line_ids % LD) < active_lines[line_ids // LD]
    rhs = (residual - coupling) * live.astype(jnp.float32)[None, None, :]
    zero_vec = jnp.zeros((NC, LINES), jnp.float32)
    last, values = lower_sweep(jac_lower, rhs, zero_vec)
    first, result = upper_sweep(jac_inv_diag, jac_upper, values, zero_vec)
    return result
```

```python
import functools

import jax
import jax.numpy as jnp
from jax import lax
from jax.experimental import pallas as pl
from jax.experimental.pallas import tpu as pltpu
from jax.sharding import PartitionSpec as P

MESH = pl.DeviceIdType.MESH
BF16 = jnp.bfloat16
F32 = jnp.float32
I32 = jnp.int32

NC = 112
LD = 128
SLOTS = 64
CH = 4
CL = LD // CH
GR = NC // CH
CR = 32


def iota(shape, dim):
    return lax.broadcasted_iota(I32, shape, dim)


def fold(rows):
    sub = iota((8, LD), 0)
    for d in (1, 2, 4):
        low = (sub & d) == 0
        rows = [
            jnp.where(low, a, b) + pltpu.roll(jnp.where(low, b, a), d, 0)
            for a, b in zip(rows[0::2], rows[1::2])
        ]
    return rows[0]


def matvec(mat_ref, vec):
    def row(j):
        return jnp.sum((mat_ref[j] * vec).reshape(NC // 8, 8, LD), axis=0)

    rows = [row(j) for j in range(GR)]
    tiles = [fold(rows[8 * t : 8 * t + 8]) for t in range(3)]
    return tiles + [fold(rows[24:28] + rows[24:28])]


def expand(tiles):
    lane = iota((8, LD), 1)
    odd = (lane // CL) % 2 == 1
    upper = lane >= 2 * CL
    top = iota((8, LD), 0) < 4
    out = [None] * 14
    for t in range(4):
        turned = [tiles[t]] + [pltpu.roll(tiles[t], CL * d, 1) for d in (1, 2, 3)]
        one = [jnp.where(odd, turned[(k + 1) % 4], turned[k]) for k in range(4)]
        two = [jnp.where(upper, one[(k + 2) % 4], one[k]) for k in range(4)]
        group = [two[(-q) % 4] for q in range(4)]
        if t < 3:
            out[4 * t : 4 * t + 4] = group
        else:
            out[12] = jnp.where(top, group[0], group[1])
            out[13] = jnp.where(top, group[2], group[3])
    return jnp.concatenate(out, 0)


def pack(ref, cell, chunk):
    group = iota((8, LD), 1) // CL
    tiles = []
    for t in range(4):
        out = None
        for q in range(4):
            tile = 4 * t + q if t < 3 else 12 + q // 2
            turned = pltpu.roll(ref[cell, pl.ds(8 * tile, 8), :], lax.rem(CL * (q - chunk) + 2 * LD, LD), 1)
            out = turned if out is None else jnp.where(group == q, turned, out)
        tiles.append(out)
    return tiles


def load_tiles(ref, *at):
    return [ref[at + (pl.ds(8 * t, 8), slice(None))] for t in range(4)]


def store_tiles(ref, tiles, *at):
    for t in range(4):
        ref[at + (pl.ds(8 * t, 8), slice(None))] = tiles[t]


def kernel(
    low_hbm, inv_hbm, upp_hbm, res_hbm, prev_hbm, sl_hbm, sc_hbm, rl_hbm, act_hbm,
    out_ref,
    stage, mats, perm, prev, res, sl, sc, rl, act,
    si, ri, gsi, gri, gp, pick, land, picked, part, pbuf,
    rhs, yin, xin, yc, xc, edge,
    stage_sem, in_sem, si_ss, si_rs, ri_ss, ri_rs, gp_ss, gp_rs, pt_ss, pt_rs, y_ss, y_rs, x_ss, x_rs,
):
    w = lax.axis_index("wall")
    span = lax.axis_index("span")
    x, z, c = span // 8, (span // 2) % 4, span % 2

    def dev(dx, dz, core):
        return (w, (dx * 4 + dz) * 2 + core)

    ring = [lambda v, d=d: lax.rem(v + d, 4) for d in (1, 2, 3)]

    smalls = [
        pltpu.make_async_copy(sl_hbm.at[0], sl, in_sem.at[0]),
        pltpu.make_async_copy(sc_hbm, sc, in_sem.at[1]),
        pltpu.make_async_copy(rl_hbm.at[0], rl, in_sem.at[2]),
        pltpu.make_async_copy(act_hbm, act, in_sem.at[3]),
        pltpu.make_async_copy(prev_hbm, prev, in_sem.at[4]),
        pltpu.make_async_copy(res_hbm, res, in_sem.at[5]),
    ]
    for copy in smalls:
        copy.start()
    sources = [low_hbm.at[0], low_hbm.at[1], upp_hbm.at[1], inv_hbm.at[1], upp_hbm.at[0], inv_hbm.at[0]]

    def stage_copy(m):
        return pltpu.make_async_copy(sources[m], stage.at[m % 3], stage_sem.at[m])

    for m in range(3):
        stage_copy(m).start()

    barrier = pltpu.get_barrier_semaphore()
    partners = [dev(turn(x), z, core) for turn in ring for core in (0, 1)]
    partners += [dev(x, turn(z), core) for turn in ring for core in (0, 1)]
    partners += [dev(x, z, 1 - c), (lax.rem(w + 1, 4), span), (lax.rem(w + 3, 4), span)]
    for partner in partners:
        pl.semaphore_signal(barrier, inc=1, device_id=partner, device_id_type=MESH)

    k = iota((512, 512), 0)
    n = iota((512, 512), 1)
    moved = (k % LD) // CL * LD + k // LD * CL + k % CL
    perm[...] = (moved == n).astype(F32).astype(BF16)

    for copy in smalls[:4]:
        copy.wait()
    active = act[0]
    diag = iota((32, 32), 0) == iota((32, 32), 1)
    count = jnp.sum(jnp.where(diag, sc[...].astype(F32), 0.0), axis=1, keepdims=True)
    lines = sl[...]
    used = (iota((32, SLOTS), 1).astype(F32) < count) & (lines < active)
    lines = jnp.where(used, lines, -1)
    recv = rl[...]

    def z_rows(values, at):
        return jnp.concatenate([values[8 * g + 2 * at : 8 * g + 2 * at + 2] for g in range(4)], 0)

    for g in range(4):
        for kind, rows in ((0, lines[8 * g : 8 * g + 8]), (4, z_rows(lines, g))):
            si[kind + g, 0:4, :] = jnp.concatenate([rows[0:4], rows[4:8]], 1)
            si[kind + g, 4:8, :] = jnp.zeros((4, LD), I32)
        for kind, rows in ((0, recv[8 * g : 8 * g + 8]), (4, z_rows(recv, g))):
            ri[kind + g] = jnp.concatenate([rows, rows], 1)

    other = 1 - c
    sends = [(dev(turn(x), z, 0), 0, turn(x), 2 * x + c) for turn in ring]
    sends += [(dev(x, turn(z), 1), 1, 4 + turn(z), 2 * z + c) for turn in ring]
    sends += [(dev(x, z, other), other, c * x + other * (4 + z), 2 * (c * x + other * z) + c)]
    marks = [(dev(x, turn(z), 0), 4 + turn(z), 2 * z + c) for turn in ring]
    marks += [(dev(turn(x), z, 1), turn(x), 2 * x + c) for turn in ring]
    marks += [(dev(x, z, other), other * x + c * (4 + z), 2 * (other * x + c * z) + c)]
    own_tile = other * x + c * (4 + z)
    own_slot = 2 * (other * x + c * z) + c
    own_mark_tile = c * x + other * (4 + z)
    own_mark = 2 * (c * x + other * z) + c

    def remote(src, dst, send_sem, recv_sem, device):
        return pltpu.make_async_remote_copy(
            src_ref=src, dst_ref=dst, send_sem=send_sem, recv_sem=recv_sem,
            device_id=device, device_id_type=MESH,
        )

    pl.semaphore_wait(barrier, len(partners))
    started = []
    for i, (device, _, tile, slot) in enumerate(sends):
        started.append(remote(si.at[tile], gsi.at[slot], si_ss.at[i], si_rs.at[slot], device))
        started[-1].start()
    for i, (device, tile, slot) in enumerate(marks):
        started.append(remote(ri.at[tile], gri.at[slot], ri_ss.at[i], ri_rs.at[slot], device))
        started[-1].start()
    smalls[4].wait()
    for i, (device, cell, _, slot) in enumerate(sends):
        started.append(remote(prev.at[cell], gp.at[slot], gp_ss.at[i], gp_rs.at[slot], device))
        started[-1].start()
    gsi[own_slot] = si[own_tile]
    gri[own_mark] = ri[own_mark_tile]
    gp[own_slot] = prev[c]

    def relayout(m):
        stage_copy(m).wait()
        source = stage.at[m % 3]
        blocks = []
        for q in range(CH):
            rows = [source[pl.ds(32 * t + 8 * q, 8)] for t in range(3)] + [source[pl.ds(96 + 4 * q, 4)]]
            blocks.append(jnp.concatenate(rows, 0).reshape(GR * NC, LD))
        turned = jnp.dot(jnp.concatenate(blocks, 1), perm[...], preferred_element_type=F32)
        for chunk in range(CH):
            mats[m, chunk] = turned[:, LD * chunk : LD * chunk + LD].reshape(GR, NC, LD)
        if m + 3 < 6:
            stage_copy(m + 3).start()

    relayout(0)

    def arrived(src, dst, recv_sem, own):
        for i in range(8):
            @pl.when(i != own)
            def _():
                remote(src, dst.at[i], si_ss.at[0], recv_sem.at[i], dev(x, z, other)).wait_recv()

    arrived(si.at[0], gsi, si_rs, own_slot)
    arrived(ri.at[0], gri, ri_rs, own_mark)
    low_lanes = iota((8, LD), 1) < SLOTS
    for s in range(8):
        for p in range(4):
            hot = iota((LD, LD), 0) == gsi[s, pl.ds(p, 1), :]
            pick[s, :, LD * p : LD * p + LD] = hot.astype(F32).astype(BF16)
    for p in range(4):
        target = jnp.where(low_lanes, gri[p], gri[p + 4] + LD)
        for s in range(8):
            hot = iota((2 * LD, LD), 0) == target[s : s + 1]
            land[p, :, LD * s : LD * s + LD] = hot.astype(F32).astype(BF16)

    arrived(prev.at[0], gp, gp_rs, own_slot)
    for s in range(8):
        value = gp[s]
        high = value.astype(BF16)
        rest = (value - high.astype(F32)).astype(BF16)
        got = jnp.dot(jnp.concatenate([high, rest], 0), pick[s], preferred_element_type=F32).astype(BF16)
        for p in range(4):
            picked[p, :, LD * s : LD * s + LD] = got[:, LD * p : LD * p + LD]
    place = other * z + c * x
    for p in range(4):
        total = lax.dot_general(picked[p], land[p], (((1,), (1,)), ((), ())), preferred_element_type=F32)
        total = total[:NC] + total[NC:]
        for h in range(2):
            part[p + 4 * h] = total[:, LD * h : LD * h + LD]
        for j in (p, p + 4):
            device = (w, other * ((x * 4 + j // 2) * 2 + j % 2) + c * (((j // 2) * 4 + z) * 2 + j % 2))

            @pl.when(j != own_mark_slot(x, z, c))
            def _():
                remote(part.at[j], pbuf.at[c, place], pt_ss.at[j], pt_rs.at[c, place], device).start()

    mine = own_mark_slot(x, z, c)
    pbuf[c, place] = part[mine]

    relayout(1)
    relayout(2)
    smalls[5].wait()

    @pl.when((w == 0) | (w == 3))
    def _():
        zero = jnp.zeros((NC, LD), F32)
        which = jnp.where(w == 0, 0, 2)

        def one(chunk, carry):
            store_tiles(edge, matvec(mats.at[which, chunk], zero), chunk)
            return carry

        lax.fori_loop(0, CH, one, 0)

    for cell in range(2):
        for slot in range(4):
            @pl.when((c != cell) | (place != slot))
            def _():
                remote(part.at[0], pbuf.at[cell, slot], pt_ss.at[0], pt_rs.at[cell, slot], dev(x, z, other)).wait_recv()

    live = (iota((NC, LD), 1) < active).astype(F32)
    for cell in range(2):
        coupling = (pbuf[cell, 0] + pbuf[cell, 1]) + (pbuf[cell, 2] + pbuf[cell, 3])
        rhs[cell] = (res[cell] - coupling) * live

    above = (lax.rem(w + 1, 4), span)
    below = (lax.rem(w + 3, 4), span)

    def y_copy(chunk):
        return remote(yc.at[1, chunk], yin.at[chunk], y_ss.at[chunk], y_rs.at[chunk], above)

    def x_copy(chunk):
        return remote(xc.at[chunk], xin.at[chunk], x_ss.at[chunk], x_rs.at[chunk], below)

    def minus(a, b):
        return [i - j for i, j in zip(a, b)]

    def forward(chunk):
        @pl.when(w > 0)
        def _():
            y_copy(chunk).wait_recv()
            store_tiles(yc, matvec(mats.at[0, chunk], expand(load_tiles(yin, chunk))), 0, chunk)

        @pl.when(w == 0)
        def _():
            store_tiles(yc, load_tiles(edge, chunk), 0, chunk)

        first = minus(pack(rhs, 0, chunk), load_tiles(yc, 0, chunk))
        store_tiles(yc, first, 0, chunk)
        second = minus(pack(rhs, 1, chunk), matvec(mats.at[1, chunk], expand(first)))
        store_tiles(yc, second, 1, chunk)

        @pl.when(w < 3)
        def _():
            y_copy(chunk).start()

    def backward(chunk):
        @pl.when(w < 3)
        def _():
            x_copy(chunk).wait_recv()
            store_tiles(xc, matvec(mats.at[2, chunk], expand(load_tiles(xin, chunk))), chunk)

        @pl.when(w == 3)
        def _():
            store_tiles(xc, load_tiles(edge, chunk), chunk)

        here = iota((NC, LD), 1) // CL == chunk
        right = minus(load_tiles(yc, 1, chunk), load_tiles(xc, chunk))
        value = expand(matvec(mats.at[3, chunk], expand(right)))
        out_ref[1] = jnp.where(here, value, out_ref[1])
        right = minus(load_tiles(yc, 0, chunk), matvec(mats.at[4, chunk], value))
        last = matvec(mats.at[5, chunk], expand(right))
        store_tiles(xc, last, chunk)

        @pl.when(w > 0)
        def _():
            x_copy(chunk).start()

        out_ref[0] = jnp.where(here, expand(last), out_ref[0])

    out_ref[...] = jnp.zeros((2, NC, LD), F32)

    def step(t, carry):
        @pl.when(t == jnp.where(w == 3, 0, CH))
        def _():
            for m in (3, 4, 5):
                relayout(m)

        is_forward = jnp.where(w == 3, t % 2 == 0, t < CH)
        chunk = jnp.where(w == 3, t // 2, t % CH)

        @pl.when(is_forward)
        def _():
            forward(chunk)

        @pl.when(jnp.logical_not(is_forward))
        def _():
            backward(chunk)

        return carry

    lax.fori_loop(0, 2 * CH, step, 0)

    for copy in started:
        copy.wait_send()
    for j in range(8):
        @pl.when(j != mine)
        def _():
            remote(part.at[j], pbuf.at[0, 0], pt_ss.at[j], pt_rs.at[0, 0], dev(x, z, other)).wait_send()

    @pl.when(w < 3)
    def _():
        for chunk in range(CH):
            y_copy(chunk).wait_send()

    @pl.when(w > 0)
    def _():
        for chunk in range(CH):
            x_copy(chunk).wait_send()


def own_mark_slot(x, z, c):
    return 2 * ((1 - c) * z + c * x) + c


def local(*args):
    dma = pltpu.SemaphoreType.DMA
    scratch = [
        pltpu.VMEM((3, NC, NC, LD), BF16),
        pltpu.VMEM((6, CH, GR, NC, LD), F32),
        pltpu.VMEM((4 * LD, 4 * LD), BF16),
        pltpu.VMEM((2, NC, LD), F32),
        pltpu.VMEM((2, NC, LD), F32),
        pltpu.VMEM((32, SLOTS), I32),
        pltpu.VMEM((1, 32), I32),
        pltpu.VMEM((32, SLOTS), I32),
        pltpu.SMEM((1,), I32),
        pltpu.VMEM((8, 8, LD), I32),
        pltpu.VMEM((8, 8, LD), I32),
        pltpu.VMEM((8, 8, LD), I32),
        pltpu.VMEM((8, 8, LD), I32),
        pltpu.VMEM((8, NC, LD), F32),
        pltpu.VMEM((8, LD, 4 * LD), BF16),
        pltpu.VMEM((4, 2 * LD, 8 * LD), BF16),
        pltpu.VMEM((4, 2 * NC, 8 * LD), BF16),
        pltpu.VMEM((8, NC, LD), F32),
        pltpu.VMEM((2, 4, NC, LD), F32),
        pltpu.VMEM((2, NC, LD), F32),
        pltpu.VMEM((CH, CR, LD), F32),
        pltpu.VMEM((CH, CR, LD), F32),
        pltpu.VMEM((2, CH, CR, LD), F32),
        pltpu.VMEM((CH, CR, LD), F32),
        pltpu.VMEM((CH, CR, LD), F32),
        dma((6,)), dma((6,)),
        dma((7,)), dma((8,)), dma((7,)), dma((8,)), dma((7,)), dma((8,)),
        dma((8,)), dma((2, 4)), dma((CH,)), dma((CH,)), dma((CH,)), dma((CH,)),
    ]
    return pl.pallas_call(
        kernel,
        out_shape=jax.ShapeDtypeStruct((2, NC, LD), F32),
        in_specs=[pl.BlockSpec(memory_space=pl.ANY)] * 9,
        out_specs=pl.BlockSpec(memory_space=pltpu.VMEM),
        scratch_shapes=scratch,
        compiler_params=pltpu.CompilerParams(
            collective_id=0, has_side_effects=True, vmem_limit_bytes=62 * 2**20
        ),
        name="relax",
    )(*args)


def solution(mesh):
    return jax.shard_map(
        local,
        mesh=mesh,
        in_specs=(
            P("wall", None, None, "span"),
            P("wall", None, None, "span"),
            P("wall", None, None, "span"),
            P("wall", None, "span"),
            P("wall", None, "span"),
            P("span", None, None),
            P("span", None),
            P("span", None, None),
            P("span"),
        ),
        out_specs=P("wall", None, "span"),
        check_vma=False,
    )
```

```python
import functools

import jax
import jax.numpy as jnp
from jax import lax
from jax.experimental import pallas as pl
from jax.experimental.pallas import tpu as pltpu
from jax.sharding import PartitionSpec as P

MESH = pl.DeviceIdType.MESH
BF16 = jnp.bfloat16
F32 = jnp.float32
I32 = jnp.int32

NC = 112
LD = 128
SLOTS = 64
CH = 4
CL = LD // CH
GR = NC // CH
CR = 32


def iota(shape, dim):
    return lax.broadcasted_iota(I32, shape, dim)


def fold(rows):
    sub = iota((8, LD), 0)
    for d in (1, 2, 4):
        low = (sub & d) == 0
        rows = [
            jnp.where(low, a, b) + pltpu.roll(jnp.where(low, b, a), d, 0)
            for a, b in zip(rows[0::2], rows[1::2])
        ]
    return rows[0]


def matvec(mat_ref, vec):
    def row(j):
        return jnp.sum((mat_ref[j] * vec).reshape(NC // 8, 8, LD), axis=0)

    rows = [row(j) for j in range(GR)]
    tiles = [fold(rows[8 * t : 8 * t + 8]) for t in range(3)]
    return tiles + [fold(rows[24:28] + rows[24:28])]


def expand(tiles):
    lane = iota((8, LD), 1)
    odd = (lane & CL) != 0
    upper = lane >= 2 * CL
    top = iota((8, LD), 0) < 4
    out = [None] * 14
    for t in range(4):
        turned = [tiles[t]] + [pltpu.roll(tiles[t], CL * d, 1) for d in (1, 2, 3)]
        one = [jnp.where(odd, turned[(k + 1) % 4], turned[k]) for k in range(4)]
        two = [jnp.where(upper, one[(k + 2) % 4], one[k]) for k in range(4)]
        group = [two[(-q) % 4] for q in range(4)]
        if t < 3:
            out[4 * t : 4 * t + 4] = group
        else:
            out[12] = jnp.where(top, group[0], group[1])
            out[13] = jnp.where(top, group[2], group[3])
    return jnp.concatenate(out, 0)


def pack(ref, cell, chunk):
    lane = iota((8, LD), 1)
    odd = (lane & CL) != 0
    upper = lane >= 2 * CL
    tiles = []
    for t in range(4):
        turned = []
        for q in range(4):
            tile = 4 * t + q if t < 3 else 12 + q // 2
            turned.append(pltpu.roll(ref[cell, pl.ds(8 * tile, 8), :], lax.rem(CL * (q - chunk) + 2 * LD, LD), 1))
        low = jnp.where(odd, turned[1], turned[0])
        high = jnp.where(odd, turned[3], turned[2])
        tiles.append(jnp.where(upper, high, low))
    return tiles


def load_tiles(ref, *at):
    return [ref[at + (pl.ds(8 * t, 8), slice(None))] for t in range(4)]


def store_tiles(ref, tiles, *at):
    for t in range(4):
        ref[at + (pl.ds(8 * t, 8), slice(None))] = tiles[t]


def kernel(
    low_hbm, inv_hbm, upp_hbm, res_hbm, prev_hbm, sl_hbm, sc_hbm, rl_hbm, act_hbm,
    out_ref,
    stage, mats, perm, prev, res, sl, sc, rl, act,
    si, ri, gsi, gri, gp, pick, land, moves, parts, part, pbuf,
    rhs, packed, yin, xin, yc, xc, upper_x, edge,
    stage_sem, in_sem, si_ss, si_rs, ri_ss, ri_rs, gp_ss, gp_rs, pt_ss, pt_rs, y_ss, y_rs, x_ss, x_rs,
):
    w = lax.axis_index("wall")
    span = lax.axis_index("span")
    x, z, c = span // 8, (span // 2) % 4, span % 2

    def dev(dx, dz, core):
        return (w, (dx * 4 + dz) * 2 + core)

    ring = [lambda v, d=d: lax.rem(v + d, 4) for d in (2, 1, 3)]

    smalls = [
        pltpu.make_async_copy(sl_hbm.at[0], sl, in_sem.at[0]),
        pltpu.make_async_copy(sc_hbm, sc, in_sem.at[1]),
        pltpu.make_async_copy(rl_hbm.at[0], rl, in_sem.at[2]),
        pltpu.make_async_copy(act_hbm, act, in_sem.at[3]),
        pltpu.make_async_copy(prev_hbm, prev, in_sem.at[4]),
        pltpu.make_async_copy(res_hbm, res, in_sem.at[5]),
    ]
    for copy in smalls:
        copy.start()
    sources = [low_hbm.at[0], low_hbm.at[1], upp_hbm.at[1], inv_hbm.at[1], upp_hbm.at[0], inv_hbm.at[0]]

    def stage_copy(m):
        return pltpu.make_async_copy(sources[m], stage.at[m % 3], stage_sem.at[m])

    for m in range(3):
        stage_copy(m).start()

    barrier = pltpu.get_barrier_semaphore()
    partners = [dev(turn(x), z, core) for turn in ring for core in (0, 1)]
    partners += [dev(x, turn(z), core) for turn in ring for core in (0, 1)]
    partners += [dev(x, z, 1 - c), (lax.rem(w + 1, 4), span), (lax.rem(w + 3, 4), span)]
    for partner in partners:
        pl.semaphore_signal(barrier, inc=1, device_id=partner, device_id_type=MESH)

    chunk_bits, line_bits = LD.bit_length() - 1, CL.bit_length() - 1
    n = iota((LD, 512), 1)
    k = iota((LD, 512), 0)
    for q in range(CH):
        moved = ((k >> line_bits) << chunk_bits) + q * CL + (k & (CL - 1))
        perm[LD * q : LD * q + LD, :] = (moved == n).astype(F32).astype(BF16)

    for copy in smalls[:4]:
        copy.wait()
    active = act[0]
    diag = iota((32, 32), 0) == iota((32, 32), 1)
    count = jnp.sum(jnp.where(diag, sc[...].astype(F32), 0.0), axis=1, keepdims=True)
    lines = sl[...]
    used = (iota((32, SLOTS), 1).astype(F32) < count) & (lines < active)
    lines = jnp.where(used, lines, -1)
    recv = rl[...]

    def z_rows(values, at):
        return jnp.concatenate([values[8 * g + 2 * at : 8 * g + 2 * at + 2] for g in range(4)], 0)

    for g in range(4):
        for kind, rows in ((0, lines[8 * g : 8 * g + 8]), (4, z_rows(lines, g))):
            si[kind + g, 0:4, :] = jnp.concatenate([rows[0:4], rows[4:8]], 1)
            si[kind + g, 4:8, :] = jnp.zeros((4, LD), I32)
        for kind, rows in ((0, recv[8 * g : 8 * g + 8]), (4, z_rows(recv, g))):
            ri[kind + g] = jnp.concatenate([rows, rows], 1)

    other = 1 - c
    sends = [(dev(turn(x), z, 0), 0, turn(x), 2 * x + c) for turn in ring]
    sends += [(dev(x, turn(z), 1), 1, 4 + turn(z), 2 * z + c) for turn in ring]
    sends += [(dev(x, z, other), other, c * x + other * (4 + z), 2 * (c * x + other * z) + c)]
    marks = [(dev(x, turn(z), 0), 4 + turn(z), 2 * z + c) for turn in ring]
    marks += [(dev(turn(x), z, 1), turn(x), 2 * x + c) for turn in ring]
    marks += [(dev(x, z, other), other * x + c * (4 + z), 2 * (other * x + c * z) + c)]
    own_tile = other * x + c * (4 + z)
    own_slot = 2 * (other * x + c * z) + c
    own_mark_tile = c * x + other * (4 + z)
    own_mark = 2 * (c * x + other * z) + c

    def remote(src, dst, send_sem, recv_sem, device):
        return pltpu.make_async_remote_copy(
            src_ref=src, dst_ref=dst, send_sem=send_sem, recv_sem=recv_sem,
            device_id=device, device_id_type=MESH,
        )

    pl.semaphore_wait(barrier, len(partners))
    started = []
    for i, (device, _, tile, slot) in enumerate(sends):
        started.append(remote(si.at[tile], gsi.at[slot], si_ss.at[i], si_rs.at[slot], device))
        started[-1].start()
    for i, (device, tile, slot) in enumerate(marks):
        started.append(remote(ri.at[tile], gri.at[slot], ri_ss.at[i], ri_rs.at[slot], device))
        started[-1].start()
    smalls[4].wait()
    for i, (device, cell, _, slot) in enumerate(sends):
        started.append(remote(prev.at[cell], gp.at[slot], gp_ss.at[i], gp_rs.at[slot], device))
        started[-1].start()
    gsi[own_slot] = si[own_tile]
    gri[own_mark] = ri[own_mark_tile]
    gp[own_slot] = prev[c]

    def relayout(m):
        stage_copy(m).wait()
        source = stage.at[m % 3]
        blocks = []
        for q in range(CH):
            rows = [source[pl.ds(32 * t + 8 * q, 8)] for t in range(3)] + [source[pl.ds(96 + 4 * q, 4)]]
            blocks.append(jnp.concatenate(rows, 0).reshape(GR * NC, LD))
        turned = jnp.dot(jnp.concatenate(blocks, 1), perm[...], preferred_element_type=F32)
        for chunk in range(CH):
            mats[m, chunk] = turned[:, LD * chunk : LD * chunk + LD].reshape(GR, NC, LD)
        if m + 3 < 6:
            stage_copy(m + 3).start()

    relayout(0)

    def arrived(src, dst, recv_sem, own):
        for i in range(8):
            @pl.when(i != own)
            def _():
                remote(src, dst.at[i], si_ss.at[0], recv_sem.at[i], dev(x, z, other)).wait_recv()

    arrived(si.at[0], gsi, si_rs, own_slot)
    arrived(ri.at[0], gri, ri_rs, own_mark)
    low_lanes = iota((8, LD), 1) < SLOTS
    for s in range(8):
        for p in range(4):
            hot = iota((LD, LD), 0) == gsi[s, pl.ds(p, 1), :]
            pick[s, :, LD * p : LD * p + LD] = hot.astype(F32).astype(BF16)
    for p in range(4):
        target = jnp.where(low_lanes, gri[p], gri[p + 4] + LD)
        for s in range(8):
            hot = iota((2 * LD, LD), 0) == target[s : s + 1]
            land[p, :, LD * s : LD * s + LD] = hot.astype(F32).astype(BF16)

    for p in range(4):
        for s in range(8):
            times = lax.dot_general(
                pick[s, :, LD * p : LD * p + LD], land[p, :, LD * s : LD * s + LD],
                (((1,), (1,)), ((), ())), preferred_element_type=F32,
            )
            moves[p, LD * s : LD * s + LD, :] = times.astype(BF16)

    arrived(prev.at[0], gp, gp_rs, own_slot)
    for s in range(8):
        value = gp[s]
        high = value.astype(BF16)
        parts[0:NC, LD * s : LD * s + LD] = high
        parts[NC : 2 * NC, LD * s : LD * s + LD] = (value - high.astype(F32)).astype(BF16)
    place = other * z + c * x
    for p in range(4):
        total = jnp.dot(parts[...], moves[p], preferred_element_type=F32)
        total = total[:NC] + total[NC:]
        for h in range(2):
            part[p + 4 * h] = total[:, LD * h : LD * h + LD]
        for j in (p, p + 4):
            device = (w, other * ((x * 4 + j // 2) * 2 + j % 2) + c * (((j // 2) * 4 + z) * 2 + j % 2))

            @pl.when(j != own_mark_slot(x, z, c))
            def _():
                remote(part.at[j], pbuf.at[c, place], pt_ss.at[j], pt_rs.at[c, place], device).start()

    mine = own_mark_slot(x, z, c)
    pbuf[c, place] = part[mine]

    relayout(1)
    relayout(2)
    smalls[5].wait()

    @pl.when((w == 0) | (w == 3))
    def _():
        zero = jnp.zeros((NC, LD), F32)
        which = jnp.where(w == 0, 0, 2)

        def one(chunk, carry):
            store_tiles(edge, matvec(mats.at[which, chunk], zero), chunk)
            return carry

        lax.fori_loop(0, CH, one, 0)

    for cell in range(2):
        for slot in range(4):
            @pl.when((c != cell) | (place != slot))
            def _():
                remote(part.at[0], pbuf.at[cell, slot], pt_ss.at[0], pt_rs.at[cell, slot], dev(x, z, other)).wait_recv()

    live = (iota((NC, LD), 1) < active).astype(F32)
    for cell in range(2):
        coupling = (pbuf[cell, 0] + pbuf[cell, 1]) + (pbuf[cell, 2] + pbuf[cell, 3])
        rhs[cell] = (res[cell] - coupling) * live

    above = (lax.rem(w + 1, 4), span)
    below = (lax.rem(w + 3, 4), span)

    def y_copy(chunk):
        return remote(yc.at[1, chunk], yin.at[chunk], y_ss.at[chunk], y_rs.at[chunk], above)

    def x_copy(chunk):
        return remote(xc.at[chunk], xin.at[chunk], x_ss.at[chunk], x_rs.at[chunk], below)

    def minus(a, b):
        return [i - j for i, j in zip(a, b)]

    def forward(chunk):
        @pl.when(w > 0)
        def _():
            y_copy(chunk).wait_recv()
            store_tiles(yc, matvec(mats.at[0, chunk], expand(load_tiles(yin, chunk))), 0, chunk)

        @pl.when(w == 0)
        def _():
            store_tiles(yc, load_tiles(edge, chunk), 0, chunk)

        first = minus(load_tiles(packed, 0, chunk), load_tiles(yc, 0, chunk))
        store_tiles(yc, first, 0, chunk)
        second = minus(load_tiles(packed, 1, chunk), matvec(mats.at[1, chunk], expand(first)))
        store_tiles(yc, second, 1, chunk)

        @pl.when(w < 3)
        def _():
            y_copy(chunk).start()

    def backward(chunk):
        @pl.when(w < 3)
        def _():
            x_copy(chunk).wait_recv()
            store_tiles(xc, matvec(mats.at[2, chunk], expand(load_tiles(xin, chunk))), chunk)

        @pl.when(w == 3)
        def _():
            store_tiles(xc, load_tiles(edge, chunk), chunk)

        right = minus(load_tiles(yc, 1, chunk), load_tiles(xc, chunk))
        value = matvec(mats.at[3, chunk], expand(right))
        store_tiles(upper_x, value, chunk)
        right = minus(load_tiles(yc, 0, chunk), matvec(mats.at[4, chunk], expand(value)))
        store_tiles(xc, matvec(mats.at[5, chunk], expand(right)), chunk)

        @pl.when(w > 0)
        def _():
            x_copy(chunk).start()

    def pack_chunk(chunk, carry):
        for cell in range(2):
            store_tiles(packed, pack(rhs, cell, chunk), cell, chunk)
        return carry

    def write_chunk(chunk, carry):
        here = (iota((NC, LD), 1) >> line_bits) == chunk
        out_ref[0] = jnp.where(here, expand(load_tiles(xc, chunk)), out_ref[0])
        out_ref[1] = jnp.where(here, expand(load_tiles(upper_x, chunk)), out_ref[1])
        return carry

    out_ref[...] = jnp.zeros((2, NC, LD), F32)

    def step(t, carry):
        @pl.when(t == jnp.where(w == 3, 0, CH))
        def _():
            for m in (3, 4, 5):
                relayout(m)

        is_forward = jnp.where(w == 3, t % 2 == 0, t < CH)
        chunk = jnp.where(w == 3, t // 2, t % CH)

        first_pack = jnp.where(w == 0, chunk, jnp.where(t == 0, 0, CH))
        last_pack = jnp.where(w == 0, jnp.where(is_forward, chunk + 1, chunk), CH)
        lax.fori_loop(first_pack, last_pack, pack_chunk, 0)

        @pl.when(is_forward)
        def _():
            forward(chunk)

        @pl.when(jnp.logical_not(is_forward))
        def _():
            backward(chunk)

        first_write = jnp.where(w == 3, jnp.where(t == 2 * CH - 1, 0, CH), chunk)
        last_write = jnp.where(w == 3, CH, jnp.where(is_forward, chunk, chunk + 1))
        lax.fori_loop(first_write, last_write, write_chunk, 0)
        return carry

    lax.fori_loop(0, 2 * CH, step, 0)

    for copy in started:
        copy.wait_send()
    for j in range(8):
        @pl.when(j != mine)
        def _():
            remote(part.at[j], pbuf.at[0, 0], pt_ss.at[j], pt_rs.at[0, 0], dev(x, z, other)).wait_send()

    @pl.when(w < 3)
    def _():
        for chunk in range(CH):
            y_copy(chunk).wait_send()

    @pl.when(w > 0)
    def _():
        for chunk in range(CH):
            x_copy(chunk).wait_send()


def own_mark_slot(x, z, c):
    return 2 * ((1 - c) * z + c * x) + c


def local(*args):
    dma = pltpu.SemaphoreType.DMA
    scratch = [
        pltpu.VMEM((3, NC, NC, LD), BF16),
        pltpu.VMEM((6, CH, GR, NC, LD), F32),
        pltpu.VMEM((4 * LD, 4 * LD), BF16),
        pltpu.VMEM((2, NC, LD), F32),
        pltpu.VMEM((2, NC, LD), F32),
        pltpu.VMEM((32, SLOTS), I32),
        pltpu.VMEM((1, 32), I32),
        pltpu.VMEM((32, SLOTS), I32),
        pltpu.SMEM((1,), I32),
        pltpu.VMEM((8, 8, LD), I32),
        pltpu.VMEM((8, 8, LD), I32),
        pltpu.VMEM((8, 8, LD), I32),
        pltpu.VMEM((8, 8, LD), I32),
        pltpu.VMEM((8, NC, LD), F32),
        pltpu.VMEM((8, LD, 4 * LD), BF16),
        pltpu.VMEM((4, 2 * LD, 8 * LD), BF16),
        pltpu.VMEM((4, 8 * LD, 2 * LD), BF16),
        pltpu.VMEM((2 * NC, 8 * LD), BF16),
        pltpu.VMEM((8, NC, LD), F32),
        pltpu.VMEM((2, 4, NC, LD), F32),
        pltpu.VMEM((2, NC, LD), F32),
        pltpu.VMEM((2, CH, CR, LD), F32),
        pltpu.VMEM((CH, CR, LD), F32),
        pltpu.VMEM((CH, CR, LD), F32),
        pltpu.VMEM((2, CH, CR, LD), F32),
        pltpu.VMEM((CH, CR, LD), F32),
        pltpu.VMEM((CH, CR, LD), F32),
        pltpu.VMEM((CH, CR, LD), F32),
        dma((6,)), dma((6,)),
        dma((7,)), dma((8,)), dma((7,)), dma((8,)), dma((7,)), dma((8,)),
        dma((8,)), dma((2, 4)), dma((CH,)), dma((CH,)), dma((CH,)), dma((CH,)),
    ]
    return pl.pallas_call(
        kernel,
        out_shape=jax.ShapeDtypeStruct((2, NC, LD), F32),
        in_specs=[pl.BlockSpec(memory_space=pl.ANY)] * 9,
        out_specs=pl.BlockSpec(memory_space=pltpu.VMEM),
        scratch_shapes=scratch,
        compiler_params=pltpu.CompilerParams(
            collective_id=0, has_side_effects=True, vmem_limit_bytes=63 * 2**20
        ),
        name="relax",
    )(*args)


def solution(mesh):
    return jax.shard_map(
        local,
        mesh=mesh,
        in_specs=(
            P("wall", None, None, "span"),
            P("wall", None, None, "span"),
            P("wall", None, None, "span"),
            P("wall", None, "span"),
            P("wall", None, "span"),
            P("span", None, None),
            P("span", None),
            P("span", None, None),
            P("span"),
        ),
        out_specs=P("wall", None, "span"),
        check_vma=False,
    )
```

```python
import functools

import jax
import jax.numpy as jnp
from jax import lax
from jax.experimental import pallas as pl
from jax.experimental.pallas import tpu as pltpu
from jax.sharding import PartitionSpec as P

MESH = pl.DeviceIdType.MESH
BF16 = jnp.bfloat16
F32 = jnp.float32
I32 = jnp.int32

NC = 112
LD = 128
SLOTS = 64
CH = 4
CL = LD // CH
GR = NC // CH
CR = 32


def iota(shape, dim):
    return lax.broadcasted_iota(I32, shape, dim)


def fold(rows):
    sub = iota((8, LD), 0)
    for d in (1, 2, 4):
        low = (sub & d) == 0
        rows = [
            jnp.where(low, a, b) + pltpu.roll(jnp.where(low, b, a), d, 0)
            for a, b in zip(rows[0::2], rows[1::2])
        ]
    return rows[0]


def matvec(mat_ref, vec):
    def row(j):
        return jnp.sum((mat_ref[j] * vec).reshape(NC // 8, 8, LD), axis=0)

    rows = [row(j) for j in range(GR)]
    tiles = [fold(rows[8 * t : 8 * t + 8]) for t in range(3)]
    return tiles + [fold(rows[24:28] + rows[24:28])]


def expand(tiles):
    lane = iota((8, LD), 1)
    odd = (lane & CL) != 0
    upper = lane >= 2 * CL
    top = iota((8, LD), 0) < 4
    out = [None] * 14
    for t in range(4):
        turned = [tiles[t]] + [pltpu.roll(tiles[t], CL * d, 1) for d in (1, 2, 3)]
        one = [jnp.where(odd, turned[(k + 1) % 4], turned[k]) for k in range(4)]
        two = [jnp.where(upper, one[(k + 2) % 4], one[k]) for k in range(4)]
        group = [two[(-q) % 4] for q in range(4)]
        if t < 3:
            out[4 * t : 4 * t + 4] = group
        else:
            out[12] = jnp.where(top, group[0], group[1])
            out[13] = jnp.where(top, group[2], group[3])
    return jnp.concatenate(out, 0)


def pack(ref, cell, chunk):
    lane = iota((8, LD), 1)
    odd = (lane & CL) != 0
    upper = lane >= 2 * CL
    tiles = []
    for t in range(4):
        turned = []
        for q in range(4):
            tile = 4 * t + q if t < 3 else 12 + q // 2
            turned.append(pltpu.roll(ref[cell, pl.ds(8 * tile, 8), :], lax.rem(CL * (q - chunk) + 2 * LD, LD), 1))
        low = jnp.where(odd, turned[1], turned[0])
        high = jnp.where(odd, turned[3], turned[2])
        tiles.append(jnp.where(upper, high, low))
    return tiles


def load_tiles(ref, *at):
    return [ref[at + (pl.ds(8 * t, 8), slice(None))] for t in range(4)]


def store_tiles(ref, tiles, *at):
    for t in range(4):
        ref[at + (pl.ds(8 * t, 8), slice(None))] = tiles[t]


def kernel(
    low_hbm, inv_hbm, upp_hbm, res_hbm, prev_hbm, sl_hbm, sc_hbm, rl_hbm, act_hbm,
    out_ref,
    stage, mats, perm, prev, res, sl, sc, rl, act,
    si, ri, gsi, gri, gp, pick, land, moves, parts, part, pbuf,
    rhs, packed, yin, xin, yc, xc, upper_x, edge,
    stage_sem, in_sem, si_ss, si_rs, ri_ss, ri_rs, gp_ss, gp_rs, pt_ss, pt_rs, y_ss, y_rs, x_ss, x_rs,
):
    w = lax.axis_index("wall")
    span = lax.axis_index("span")
    x, z, c = span // 8, (span // 2) % 4, span % 2

    def dev(dx, dz, core):
        return (w, (dx * 4 + dz) * 2 + core)

    ring = [lambda v, d=d: lax.rem(v + d, 4) for d in (2, 1, 3)]

    barrier = pltpu.get_barrier_semaphore()
    partners = [dev(turn(x), z, core) for turn in ring for core in (0, 1)]
    partners += [dev(x, turn(z), core) for turn in ring for core in (0, 1)]
    partners += [dev(x, z, 1 - c), (lax.rem(w + 1, 4), span), (lax.rem(w + 3, 4), span)]
    for partner in partners:
        pl.semaphore_signal(barrier, inc=1, device_id=partner, device_id_type=MESH)

    smalls = [
        pltpu.make_async_copy(sl_hbm.at[0], sl, in_sem.at[0]),
        pltpu.make_async_copy(sc_hbm, sc, in_sem.at[1]),
        pltpu.make_async_copy(rl_hbm.at[0], rl, in_sem.at[2]),
        pltpu.make_async_copy(act_hbm, act, in_sem.at[3]),
        pltpu.make_async_copy(prev_hbm, prev, in_sem.at[4]),
        pltpu.make_async_copy(res_hbm, res, in_sem.at[5]),
    ]
    for copy in smalls:
        copy.start()
    sources = [low_hbm.at[0], low_hbm.at[1], upp_hbm.at[1], inv_hbm.at[1], upp_hbm.at[0], inv_hbm.at[0]]

    def stage_copy(m):
        return pltpu.make_async_copy(sources[m], stage.at[m % 3], stage_sem.at[m])


    chunk_bits, line_bits = LD.bit_length() - 1, CL.bit_length() - 1
    n = iota((LD, 512), 1)
    k = iota((LD, 512), 0)
    for q in range(CH):
        moved = ((k >> line_bits) << chunk_bits) + q * CL + (k & (CL - 1))
        perm[LD * q : LD * q + LD, :] = (moved == n).astype(F32).astype(BF16)

    for copy in smalls[:4]:
        copy.wait()
    active = act[0]
    diag = iota((32, 32), 0) == iota((32, 32), 1)
    count = jnp.sum(jnp.where(diag, sc[...].astype(F32), 0.0), axis=1, keepdims=True)
    lines = sl[...]
    used = (iota((32, SLOTS), 1).astype(F32) < count) & (lines < active)
    lines = jnp.where(used, lines, -1)
    recv = rl[...]

    def z_rows(values, at):
        return jnp.concatenate([values[8 * g + 2 * at : 8 * g + 2 * at + 2] for g in range(4)], 0)

    for g in range(4):
        for kind, rows in ((0, lines[8 * g : 8 * g + 8]), (4, z_rows(lines, g))):
            si[kind + g, 0:4, :] = jnp.concatenate([rows[0:4], rows[4:8]], 1)
            si[kind + g, 4:8, :] = jnp.zeros((4, LD), I32)
        for kind, rows in ((0, recv[8 * g : 8 * g + 8]), (4, z_rows(recv, g))):
            ri[kind + g] = jnp.concatenate([rows, rows], 1)

    other = 1 - c
    sends = [(dev(turn(x), z, 0), 0, turn(x), 2 * x + c) for turn in ring]
    sends += [(dev(x, turn(z), 1), 1, 4 + turn(z), 2 * z + c) for turn in ring]
    sends += [(dev(x, z, other), other, c * x + other * (4 + z), 2 * (c * x + other * z) + c)]
    marks = [(dev(x, turn(z), 0), 4 + turn(z), 2 * z + c) for turn in ring]
    marks += [(dev(turn(x), z, 1), turn(x), 2 * x + c) for turn in ring]
    marks += [(dev(x, z, other), other * x + c * (4 + z), 2 * (other * x + c * z) + c)]
    own_tile = other * x + c * (4 + z)
    own_slot = 2 * (other * x + c * z) + c
    own_mark_tile = c * x + other * (4 + z)
    own_mark = 2 * (c * x + other * z) + c

    def remote(src, dst, send_sem, recv_sem, device):
        return pltpu.make_async_remote_copy(
            src_ref=src, dst_ref=dst, send_sem=send_sem, recv_sem=recv_sem,
            device_id=device, device_id_type=MESH,
        )

    for m in range(3):
        stage_copy(m).start()

    pl.semaphore_wait(barrier, len(partners))
    started = []
    for i, (device, _, tile, slot) in enumerate(sends):
        started.append(remote(si.at[tile], gsi.at[slot], si_ss.at[i], si_rs.at[slot], device))
        started[-1].start()
    for i, (device, tile, slot) in enumerate(marks):
        started.append(remote(ri.at[tile], gri.at[slot], ri_ss.at[i], ri_rs.at[slot], device))
        started[-1].start()
    smalls[4].wait()
    for i, (device, cell, _, slot) in enumerate(sends):
        started.append(remote(prev.at[cell], gp.at[slot], gp_ss.at[i], gp_rs.at[slot], device))
        started[-1].start()
    gsi[own_slot] = si[own_tile]
    gri[own_mark] = ri[own_mark_tile]
    gp[own_slot] = prev[c]

    def relayout(m):
        stage_copy(m).wait()
        source = stage.at[m % 3]
        blocks = []
        for q in range(CH):
            rows = [source[pl.ds(32 * t + 8 * q, 8)] for t in range(3)] + [source[pl.ds(96 + 4 * q, 4)]]
            blocks.append(jnp.concatenate(rows, 0).reshape(GR * NC, LD))
        turned = jnp.dot(jnp.concatenate(blocks, 1), perm[...], preferred_element_type=F32)
        for chunk in range(CH):
            mats[m, chunk] = turned[:, LD * chunk : LD * chunk + LD].reshape(GR, NC, LD)
        if m + 3 < 6:
            stage_copy(m + 3).start()

    relayout(0)

    def arrived(src, dst, recv_sem, own):
        for i in range(8):
            @pl.when(i != own)
            def _():
                remote(src, dst.at[i], si_ss.at[0], recv_sem.at[i], dev(x, z, other)).wait_recv()

    arrived(si.at[0], gsi, si_rs, own_slot)
    arrived(ri.at[0], gri, ri_rs, own_mark)
    low_lanes = iota((8, LD), 1) < SLOTS
    for s in range(8):
        for p in range(4):
            hot = iota((LD, LD), 0) == gsi[s, pl.ds(p, 1), :]
            pick[s, :, LD * p : LD * p + LD] = hot.astype(F32).astype(BF16)
    for p in range(4):
        target = jnp.where(low_lanes, gri[p], gri[p + 4] + LD)
        for s in range(8):
            hot = iota((2 * LD, LD), 0) == target[s : s + 1]
            land[p, :, LD * s : LD * s + LD] = hot.astype(F32).astype(BF16)

    for p in range(4):
        for s in range(8):
            times = lax.dot_general(
                pick[s, :, LD * p : LD * p + LD], land[p, :, LD * s : LD * s + LD],
                (((1,), (1,)), ((), ())), preferred_element_type=F32,
            )
            moves[p, LD * s : LD * s + LD, :] = times.astype(BF16)

    arrived(prev.at[0], gp, gp_rs, own_slot)
    for s in range(8):
        value = gp[s]
        high = value.astype(BF16)
        parts[0:NC, LD * s : LD * s + LD] = high
        parts[NC : 2 * NC, LD * s : LD * s + LD] = (value - high.astype(F32)).astype(BF16)
    place = other * z + c * x
    for p in range(4):
        total = jnp.dot(parts[...], moves[p], preferred_element_type=F32)
        total = total[:NC] + total[NC:]
        for h in range(2):
            part[p + 4 * h] = total[:, LD * h : LD * h + LD]
        for j in (p, p + 4):
            device = (w, other * ((x * 4 + j // 2) * 2 + j % 2) + c * (((j // 2) * 4 + z) * 2 + j % 2))

            @pl.when(j != own_mark_slot(x, z, c))
            def _():
                remote(part.at[j], pbuf.at[c, place], pt_ss.at[j], pt_rs.at[c, place], device).start()

    mine = own_mark_slot(x, z, c)
    pbuf[c, place] = part[mine]

    relayout(1)
    relayout(2)
    smalls[5].wait()

    @pl.when((w == 0) | (w == 3))
    def _():
        zero = jnp.zeros((NC, LD), F32)
        which = jnp.where(w == 0, 0, 2)

        def one(chunk, carry):
            store_tiles(edge, matvec(mats.at[which, chunk], zero), chunk)
            return carry

        lax.fori_loop(0, CH, one, 0)

    for cell in range(2):
        for slot in range(4):
            @pl.when((c != cell) | (place != slot))
            def _():
                remote(part.at[0], pbuf.at[cell, slot], pt_ss.at[0], pt_rs.at[cell, slot], dev(x, z, other)).wait_recv()

    live = (iota((NC, LD), 1) < active).astype(F32)
    for cell in range(2):
        coupling = (pbuf[cell, 0] + pbuf[cell, 1]) + (pbuf[cell, 2] + pbuf[cell, 3])
        rhs[cell] = (res[cell] - coupling) * live

    above = (lax.rem(w + 1, 4), span)
    below = (lax.rem(w + 3, 4), span)

    def y_copy(chunk):
        return remote(yc.at[1, chunk], yin.at[chunk], y_ss.at[chunk], y_rs.at[chunk], above)

    def x_copy(chunk):
        return remote(xc.at[chunk], xin.at[chunk], x_ss.at[chunk], x_rs.at[chunk], below)

    def minus(a, b):
        return [i - j for i, j in zip(a, b)]

    def forward(chunk):
        @pl.when(w > 0)
        def _():
            y_copy(chunk).wait_recv()
            store_tiles(yc, matvec(mats.at[0, chunk], expand(load_tiles(yin, chunk))), 0, chunk)

        @pl.when(w == 0)
        def _():
            store_tiles(yc, load_tiles(edge, chunk), 0, chunk)

        first = minus(load_tiles(packed, 0, chunk), load_tiles(yc, 0, chunk))
        store_tiles(yc, first, 0, chunk)
        second = minus(load_tiles(packed, 1, chunk), matvec(mats.at[1, chunk], expand(first)))
        store_tiles(yc, second, 1, chunk)

        @pl.when(w < 3)
        def _():
            y_copy(chunk).start()

    def backward(chunk):
        @pl.when(w < 3)
        def _():
            x_copy(chunk).wait_recv()
            store_tiles(xc, matvec(mats.at[2, chunk], expand(load_tiles(xin, chunk))), chunk)

        @pl.when(w == 3)
        def _():
            store_tiles(xc, load_tiles(edge, chunk), chunk)

        right = minus(load_tiles(yc, 1, chunk), load_tiles(xc, chunk))
        value = matvec(mats.at[3, chunk], expand(right))
        store_tiles(upper_x, value, chunk)
        right = minus(load_tiles(yc, 0, chunk), matvec(mats.at[4, chunk], expand(value)))
        store_tiles(xc, matvec(mats.at[5, chunk], expand(right)), chunk)

        @pl.when(w > 0)
        def _():
            x_copy(chunk).start()

    def both(chunk):
        y_copy(chunk).wait_recv()
        done = chunk - 1
        right = minus(load_tiles(yc, 1, done), load_tiles(edge, done))
        lower = load_tiles(yc, 0, done)
        ahead = load_tiles(packed, 0, chunk), load_tiles(packed, 1, chunk)
        enter = matvec(mats.at[0, chunk], expand(load_tiles(yin, chunk)))
        value = matvec(mats.at[3, done], expand(right))
        first = minus(ahead[0], enter)
        between = matvec(mats.at[1, chunk], expand(first))
        back = matvec(mats.at[4, done], expand(value))
        second = minus(ahead[1], between)
        last = matvec(mats.at[5, done], expand(minus(lower, back)))
        store_tiles(xc, last, done)
        x_copy(done).start()
        store_tiles(upper_x, value, done)
        store_tiles(yc, first, 0, chunk)
        store_tiles(yc, second, 1, chunk)

    def pack_chunk(chunk, carry):
        for cell in range(2):
            store_tiles(packed, pack(rhs, cell, chunk), cell, chunk)
        return carry

    def write_chunk(chunk, carry):
        here = (iota((NC, LD), 1) >> line_bits) == chunk
        out_ref[0] = jnp.where(here, expand(load_tiles(xc, chunk)), out_ref[0])
        out_ref[1] = jnp.where(here, expand(load_tiles(upper_x, chunk)), out_ref[1])
        return carry

    out_ref[...] = jnp.zeros((2, NC, LD), F32)

    def step(t, carry):
        @pl.when(t == jnp.where(w >= 2, 0, CH))
        def _():
            for m in (3, 4, 5):
                relayout(m)

        is_forward = t < jnp.where(w == 3, 1, CH)
        is_both = (w == 3) & (t > 0) & (t < CH)
        is_backward = (t >= CH) & (t < jnp.where(w == 3, CH + 1, 2 * CH))
        chunk = jnp.where(w == 3, jnp.where(t == 0, 0, CH - 1), t % CH)

        first_pack = jnp.where(w == 0, chunk, jnp.where(t == 0, 0, CH))
        last_pack = jnp.where(w == 0, jnp.where(is_forward, chunk + 1, chunk), CH)
        lax.fori_loop(first_pack, last_pack, pack_chunk, 0)

        @pl.when(is_forward)
        def _():
            forward(chunk)

        @pl.when(is_both)
        def _():
            both(t)

        @pl.when(is_backward)
        def _():
            backward(chunk)

        first_write = jnp.where(w == 3, jnp.where(t == CH, 0, CH), chunk)
        last_write = jnp.where(w == 3, CH, jnp.where(is_forward, chunk, chunk + 1))
        lax.fori_loop(first_write, last_write, write_chunk, 0)
        return carry

    lax.fori_loop(0, 2 * CH, step, 0)

    for copy in started:
        copy.wait_send()
    for j in range(8):
        @pl.when(j != mine)
        def _():
            remote(part.at[j], pbuf.at[0, 0], pt_ss.at[j], pt_rs.at[0, 0], dev(x, z, other)).wait_send()

    @pl.when(w < 3)
    def _():
        for chunk in range(CH):
            y_copy(chunk).wait_send()

    @pl.when(w > 0)
    def _():
        for chunk in range(CH):
            x_copy(chunk).wait_send()


def own_mark_slot(x, z, c):
    return 2 * ((1 - c) * z + c * x) + c


def local(*args):
    dma = pltpu.SemaphoreType.DMA
    scratch = [
        pltpu.VMEM((3, NC, NC, LD), BF16),
        pltpu.VMEM((6, CH, GR, NC, LD), F32),
        pltpu.VMEM((4 * LD, 4 * LD), BF16),
        pltpu.VMEM((2, NC, LD), F32),
        pltpu.VMEM((2, NC, LD), F32),
        pltpu.VMEM((32, SLOTS), I32),
        pltpu.VMEM((1, 32), I32),
        pltpu.VMEM((32, SLOTS), I32),
        pltpu.SMEM((1,), I32),
        pltpu.VMEM((8, 8, LD), I32),
        pltpu.VMEM((8, 8, LD), I32),
        pltpu.VMEM((8, 8, LD), I32),
        pltpu.VMEM((8, 8, LD), I32),
        pltpu.VMEM((8, NC, LD), F32),
        pltpu.VMEM((8, LD, 4 * LD), BF16),
        pltpu.VMEM((4, 2 * LD, 8 * LD), BF16),
        pltpu.VMEM((4, 8 * LD, 2 * LD), BF16),
        pltpu.VMEM((2 * NC, 8 * LD), BF16),
        pltpu.VMEM((8, NC, LD), F32),
        pltpu.VMEM((2, 4, NC, LD), F32),
        pltpu.VMEM((2, NC, LD), F32),
        pltpu.VMEM((2, CH, CR, LD), F32),
        pltpu.VMEM((CH, CR, LD), F32),
        pltpu.VMEM((CH, CR, LD), F32),
        pltpu.VMEM((2, CH, CR, LD), F32),
        pltpu.VMEM((CH, CR, LD), F32),
        pltpu.VMEM((CH, CR, LD), F32),
        pltpu.VMEM((CH, CR, LD), F32),
        dma((6,)), dma((6,)),
        dma((7,)), dma((8,)), dma((7,)), dma((8,)), dma((7,)), dma((8,)),
        dma((8,)), dma((2, 4)), dma((CH,)), dma((CH,)), dma((CH,)), dma((CH,)),
    ]
    return pl.pallas_call(
        kernel,
        out_shape=jax.ShapeDtypeStruct((2, NC, LD), F32),
        in_specs=[pl.BlockSpec(memory_space=pl.ANY)] * 9,
        out_specs=pl.BlockSpec(memory_space=pltpu.VMEM),
        scratch_shapes=scratch,
        compiler_params=pltpu.CompilerParams(
            collective_id=0, has_side_effects=True, vmem_limit_bytes=63 * 2**20
        ),
        name="relax",
    )(*args)


def solution(mesh):
    return jax.shard_map(
        local,
        mesh=mesh,
        in_specs=(
            P("wall", None, None, "span"),
            P("wall", None, None, "span"),
            P("wall", None, None, "span"),
            P("wall", None, "span"),
            P("wall", None, "span"),
            P("span", None, None),
            P("span", None),
            P("span", None, None),
            P("span"),
        ),
        out_specs=P("wall", None, "span"),
        check_vma=False,
    )
```
